32 devices in a mesh: gy: 16 (over z, x, core), gz: 2 (over y).
Axes of the slice: x: 2, y: 2, z: 4, core: 2. Of those that a mesh axis runs over, the one named last changes fastest.
Arguments:
- level_set: float32 [16, 256, 2048], P('gz', 'gy'), may hold values from -6 to 6
- velocity: float32 [3, 16, 256, 2048], P(None, 'gz', 'gy'), may hold values from -6 to 6
Outputs:
- force: float32 [3, 16, 256, 2048], P(None, 'gz', 'gy')
- spectrum: float32 [16, 2, 1024, 256], P('gz', None, 'gy')
The draws below stay inside these ranges and needn't reach their ends.
All inputs are finite; a program needn't handle non-finite values.
Results may differ from the reference program's by a relative error of at most 0.00007.
Values sent between devices are 32-bit elements; how exact they have to be, the bound alone decides.
A program may use at most 128 MiB of HBM per device.

```python
import math
import jax
import jax.numpy as jnp
from jax import lax

X = 2048
Y = 256
NZ = 16


def levels(rng, extent, cuts, low, largest):
    level, own = 1.0, jax.random.fold_in(rng, 6)
    for position, shards_of in cuts:
        heights = jnp.exp(jax.random.uniform(jax.random.fold_in(own, position), (shards_of,), jnp.float32, low / len(cuts), largest / len(cuts)))
        level = level * jnp.repeat(heights, extent[position] // shards_of).reshape([-1 if axis == position else 1 for axis in range(len(extent))])
    return level


def noise(key, dims, scale, most, pieces=(), held_as=jnp.bfloat16):
    entries = scale * jax.random.normal(key, dims, jnp.float32)
    if pieces:
        entries = entries * levels(key, dims, pieces, -0.22, 0.18)
    return jnp.clip(entries, -most, most).astype(held_as)


def setup_inputs(seed: int = 0) -> dict:
    key_of = jax.random.split(jax.random.key(seed), 3)
    return {
        "level_set": noise(key_of[0], (NZ, Y, X), 1.0, 6.0, ((0, 2), (1, 16)), jnp.float32),
        "velocity": noise(key_of[1], (3, NZ, Y, X), 1.0, 6.0, ((1, 2), (2, 16)), jnp.float32),
    }


surface_tension = 1.0
time_step = 0.5

def slope_depth(field):
    return (field[..., 2:, :, :] - field[..., :-2, :, :]) * 0.5

def slope_span(field):
    return ((jnp.roll(field, -1, -2) - jnp.roll(field, 1, -2)) * 0.5)[..., 1:-1, :, :]

def slope_line(field):
    return ((jnp.roll(field, -1, -1) - jnp.roll(field, 1, -1)) * 0.5)[..., 1:-1, :, :]

def normals_from(level):
    grad_x = slope_line(level)
    grad_y = slope_span(level)
    grad_z = slope_depth(level)
    scale = jnp.sqrt(grad_x * grad_x + grad_y * grad_y + grad_z * grad_z + 1.0)
    return jnp.stack([grad_x / scale, grad_y / scale, grad_z / scale])

def divergence(field):
    return slope_line(field[0]) + slope_span(field[1]) + slope_depth(field[2])

def heavy_slopes(level):
    heavy = 0.5 * (1.0 + jnp.tanh(level))
    return jnp.stack([slope_line(heavy), slope_span(heavy), slope_depth(heavy)])

def reference(level_set, velocity):
    level_pad = jnp.concatenate([level_set[-3:], level_set, level_set[:3]], axis=0)
    vel_pad = jnp.concatenate([velocity[:, -1:], velocity, velocity[:, :1]], axis=1)

    def plane(center):
        window = lax.dynamic_slice_in_dim(level_pad, center, 7, 0)
        vel_window = lax.dynamic_slice_in_dim(vel_pad, center, 3, 1)
        normal = normals_from(window)
        kappa = -divergence(normal)
        slopes = heavy_slopes(window[1:-1])
        force_wide = surface_tension * kappa * slopes
        source = (divergence(vel_window) + time_step * divergence(force_wide))[0]
        spec = jnp.fft.rfft(source, axis=-1) / math.sqrt(X)
        real_part = jnp.real(spec)[:, :X // 2]
        imag_part = jnp.imag(spec)[:, :X // 2]
        imag_part = imag_part.at[:, 0].set(jnp.real(spec)[:, X // 2])
        packed = real_part + 1j * imag_part
        lines_out = jnp.fft.fft(packed, axis=0) / math.sqrt(Y)
        planar = jnp.stack([jnp.real(lines_out).T, jnp.imag(lines_out).T]).astype(jnp.float32)
        return (force_wide[:, 1].astype(jnp.float32), planar)
    forces, spectra = lax.map(plane, jnp.arange(NZ, dtype=jnp.int32))
    return (jnp.moveaxis(forces, 0, 1), spectra)
```

```python
import functools
import math

import jax
import jax.numpy as jnp
import ml_dtypes
import numpy as np
from jax import lax
from jax.experimental import pallas as pl
from jax.experimental.pallas import tpu as pltpu
from jax.sharding import PartitionSpec as P

X = 2048


surface_tension = 1.0
time_step = 0.5


def padded_2(cells, sides, width):
    for axis, dim in sides:
        count = lax.axis_size(axis)
        head = lax.slice_in_dim(cells, 0, width, axis=dim)
        tail = lax.slice_in_dim(cells, cells.shape[dim] - width, cells.shape[dim], axis=dim)
        cells = jnp.concatenate(
            [
                lax.ppermute(tail, axis, [(i, (i + 1) % count) for i in range(count)]),
                cells,
                lax.ppermute(head, axis, [((i + 1) % count, i) for i in range(count)]),
            ],
            axis=dim,
        )
    return cells


def slope_depth(field):
    return (field[..., 2:, 1:-1, :] - field[..., :-2, 1:-1, :]) * 0.5


def slope_span(field):
    return (field[..., 1:-1, 2:, :] - field[..., 1:-1, :-2, :]) * 0.5


def slope_line(field):
    inner = field[..., 1:-1, 1:-1, :]
    return (jnp.roll(inner, -1, -1) - jnp.roll(inner, 1, -1)) * 0.5


def normals_from(level):
    grad_x = slope_line(level)
    grad_y = slope_span(level)
    grad_z = slope_depth(level)
    scale = jnp.sqrt(grad_x * grad_x + grad_y * grad_y + grad_z * grad_z + 1.0)
    return jnp.stack([grad_x / scale, grad_y / scale, grad_z / scale])


def divergence(field):
    return slope_line(field[0]) + slope_span(field[1]) + slope_depth(field[2])


def heavy_slopes(level):
    heavy = 0.5 * (1.0 + jnp.tanh(level))
    return jnp.stack([slope_line(heavy), slope_span(heavy), slope_depth(heavy)])


MESH = pl.DeviceIdType.MESH


def halves(table):
    high = table.astype(np.float32).astype(ml_dtypes.bfloat16)
    low = (table - high.astype(np.float64)).astype(np.float32).astype(ml_dtypes.bfloat16)
    return np.stack([high, low])


def line_tables(line, peers):
    position = np.arange(line)[:, None]
    wavenum = np.arange(line // 2)[None, :]
    phase = (position * wavenum % line) * (2.0 * math.pi / line)
    nyquist = np.where(position % 2 == 0, 1.0, -1.0)
    second = np.where(wavenum == 0, nyquist, -np.sin(phase))
    table = np.stack([np.cos(phase), second], axis=1) / math.sqrt(line)
    own = line // 2 // peers
    table = table.reshape(line, 2, peers, own).transpose(2, 0, 1, 3).reshape(peers, line, 2 * own)
    table = table.reshape(peers // 2, 2, line, 2 * own).transpose(0, 2, 1, 3)
    return halves(table.reshape(peers // 2, line, 4 * own))


def span_tables(span):
    index = np.arange(span)
    phase = (index[:, None] * index[None, :] % span) * (2.0 * math.pi / span)
    return halves(np.concatenate([np.cos(phase), np.sin(phase)], axis=1) / math.sqrt(span))


def split(value):
    high = value.astype(jnp.bfloat16)
    return high, (value - high.astype(jnp.float32)).astype(jnp.bfloat16)


def dot3(left, high, low):
    rows = left.shape[0]
    first, rest = split(left)
    both = jnp.dot(jnp.concatenate([first, rest], axis=0), high, preferred_element_type=jnp.float32)
    return both[:rows] + both[rows:] + jnp.dot(first, low, preferred_element_type=jnp.float32)


def chip_order(chips):
    return sorted(range(1, chips), key=lambda off: (abs(off - chips // 2), off))


def spectrum_kernel(peers, source_ref, line_hbm, span_ref, out_ref, line_tab, sent, got, tab_sem, send_sem, recv_sem):
    me = lax.axis_index("gy")
    chips = peers // 2
    chip = me // 2
    core = me % 2
    offsets = chip_order(chips) + [0]
    loads = []
    for step, off in enumerate(offsets):
        target = (chip + off) % chips
        load = pltpu.make_async_copy(line_hbm.at[:, target], line_tab.at[step], tab_sem.at[step])
        load.start()
        loads.append(load)

    barrier = pltpu.get_barrier_semaphore()
    for off in range(1, peers):
        pl.semaphore_signal(barrier, inc=1, device_id={"gy": (me + off) % peers}, device_id_type=MESH)
    pl.semaphore_wait(barrier, peers - 1)

    depth, span, line = source_ref.shape
    copies = []
    for step, off in enumerate(offsets):
        loads[step].wait()
        target = (chip + off) % chips
        block = dot3(source_ref[...].reshape(depth * span, line), line_tab[step, 0], line_tab[step, 1])
        half = block.shape[1] // 2
        for side in range(2):
            sent[step, side] = block[:, side * half:(side + 1) * half].reshape(depth, span, half)
        if off:
            for side in range(2):
                copy = pltpu.make_async_remote_copy(
                    src_ref=sent.at[step, side], dst_ref=got.at[me],
                    send_sem=send_sem.at[2 * step + side], recv_sem=recv_sem.at[me],
                    device_id={"gy": 2 * target + side}, device_id_type=MESH)
                copy.start()
                copies.append(copy)
        else:
            copy = pltpu.make_async_remote_copy(
                src_ref=sent.at[step, 1 - core], dst_ref=got.at[me],
                send_sem=send_sem.at[2 * step], recv_sem=recv_sem.at[me],
                device_id={"gy": 2 * chip + 1 - core}, device_id_type=MESH)
            copy.start()
            copies.append(copy)
            got[me] = sent[step, core]
    for off in range(1, peers):
        source = (me + off) % peers
        pltpu.make_async_remote_copy(
            src_ref=sent.at[0, 0], dst_ref=got.at[source],
            send_sem=send_sem.at[0], recv_sem=recv_sem.at[source],
            device_id={"gy": source}, device_id_type=MESH).wait_recv()
    total = peers * span
    for layer in range(depth):
        lines = got[:, layer].reshape(total, -1).T
        own = lines.shape[0] // 2
        product = dot3(lines, span_ref[0], span_ref[1])
        out_ref[layer, 0] = product[:own, :total] + product[own:, total:]
        out_ref[layer, 1] = product[own:, :total] - product[:own, total:]
    for copy in copies:
        copy.wait_send()


def spectrum_by_kernel(source, peers):
    depth, span, line = source.shape
    own = line // 2 // peers
    vmem = pl.BlockSpec(memory_space=pltpu.VMEM)
    return pl.pallas_call(
        functools.partial(spectrum_kernel, peers),
        out_shape=jax.ShapeDtypeStruct((depth, 2, own, peers * span), jnp.float32),
        in_specs=[vmem, pl.BlockSpec(memory_space=pl.ANY), vmem],
        out_specs=vmem,
        scratch_shapes=[
            pltpu.VMEM((peers // 2, 2, line, 4 * own), jnp.bfloat16),
            pltpu.VMEM((peers // 2, 2, depth, span, 2 * own), jnp.float32),
            pltpu.VMEM((peers, depth, span, 2 * own), jnp.float32),
            pltpu.SemaphoreType.DMA((peers // 2,)),
            pltpu.SemaphoreType.DMA((peers,)),
            pltpu.SemaphoreType.DMA((peers,)),
        ],
        compiler_params=pltpu.CompilerParams(
            collective_id=0, has_side_effects=True, vmem_limit_bytes=56 * 2**20),
    )(source, jnp.asarray(line_tables(line, peers)), jnp.asarray(span_tables(peers * span)))


def on_device(level_set, velocity):
    padded = padded_2(level_set, (("gy", 1), ("gz", 0)), 3)
    vel_wide = padded_2(velocity, (("gy", 2), ("gz", 1)), 1)
    kappa = -divergence(normals_from(padded))
    force_wide = surface_tension * kappa * heavy_slopes(padded[1:-1, 1:-1])
    force_own = force_wide[:, 1:-1, 1:-1]
    div_force = divergence(force_wide)
    source = divergence(vel_wide) + time_step * div_force
    peers = lax.axis_size("gy")
    if peers % 2 == 0 and source.shape[2] == 64 * peers * 2 and source.shape[1] % 8 == 0:
        return (force_own, spectrum_by_kernel(source, peers))
    depth_cells = source.shape[0]
    span_cells = source.shape[1]
    half_len = X // 2
    span_total = span_cells * lax.axis_size("gy")
    position = jnp.arange(X, dtype=jnp.int32)[:, None]
    wavenum = jnp.arange(half_len, dtype=jnp.int32)[None, :]
    phase = (position * wavenum % X).astype(jnp.float32) * (2.0 * math.pi / X)
    nyquist = jnp.where(position % 2 == 0, 1.0, -1.0).astype(jnp.float32)
    second = jnp.where(wavenum == 0, nyquist, -jnp.sin(phase))
    line_table = (jnp.stack([jnp.cos(phase), second], axis=1) / math.sqrt(X)).reshape(X, X)
    transformed = jnp.dot(
        source.reshape(-1, X),
        line_table,
        precision=lax.Precision.HIGHEST,
        preferred_element_type=jnp.float32,
    )
    transformed = transformed.reshape(depth_cells, span_cells, 2, half_len)
    rows_index = jnp.arange(span_total, dtype=jnp.int32)[:, None]
    cols_index = jnp.arange(span_total, dtype=jnp.int32)[None, :]
    span_phase = (rows_index * cols_index % span_total).astype(jnp.float32) * (
        2.0 * math.pi / span_total
    )
    span_cos = jnp.cos(span_phase) / math.sqrt(span_total)
    span_sin = jnp.sin(span_phase) / math.sqrt(span_total)
    piece = lax.all_to_all(transformed, "gy", split_axis=3, concat_axis=1, tiled=True)
    first = piece[:, :, 0, :]
    other = piece[:, :, 1, :]
    high = lax.Precision.HIGHEST
    first_cos = jnp.einsum("nyk,yq->nkq", first, span_cos, precision=high)
    first_sin = jnp.einsum("nyk,yq->nkq", first, span_sin, precision=high)
    other_cos = jnp.einsum("nyk,yq->nkq", other, span_cos, precision=high)
    other_sin = jnp.einsum("nyk,yq->nkq", other, span_sin, precision=high)
    spectrum = jnp.stack([first_cos + other_sin, other_cos - first_sin], axis=1)
    return (force_own, spectrum)


def solution(mesh):
    placed = (P("gz", "gy", None), P(None, "gz", "gy", None))
    return jax.shard_map(
        on_device,
        mesh=mesh,
        in_specs=placed,
        out_specs=(P(None, "gz", "gy", None), P("gz", None, "gy", None)),
        check_vma=False,
    )
```

```python
import functools
import math

import jax
import jax.numpy as jnp
import ml_dtypes
import numpy as np
from jax import lax
from jax.experimental import pallas as pl
from jax.experimental.pallas import tpu as pltpu
from jax.sharding import PartitionSpec as P

X = 2048


surface_tension = 1.0
time_step = 0.5


def padded_2(cells, sides, width):
    for axis, dim in sides:
        count = lax.axis_size(axis)
        head = lax.slice_in_dim(cells, 0, width, axis=dim)
        tail = lax.slice_in_dim(cells, cells.shape[dim] - width, cells.shape[dim], axis=dim)
        cells = jnp.concatenate(
            [
                lax.ppermute(tail, axis, [(i, (i + 1) % count) for i in range(count)]),
                cells,
                lax.ppermute(head, axis, [((i + 1) % count, i) for i in range(count)]),
            ],
            axis=dim,
        )
    return cells


def slope_depth(field):
    return (field[..., 2:, 1:-1, :] - field[..., :-2, 1:-1, :]) * 0.5


def slope_span(field):
    return (field[..., 1:-1, 2:, :] - field[..., 1:-1, :-2, :]) * 0.5


def slope_line(field):
    inner = field[..., 1:-1, 1:-1, :]
    return (jnp.roll(inner, -1, -1) - jnp.roll(inner, 1, -1)) * 0.5


def normals_from(level):
    grad_x = slope_line(level)
    grad_y = slope_span(level)
    grad_z = slope_depth(level)
    scale = jnp.sqrt(grad_x * grad_x + grad_y * grad_y + grad_z * grad_z + 1.0)
    return jnp.stack([grad_x / scale, grad_y / scale, grad_z / scale])


def divergence(field):
    return slope_line(field[0]) + slope_span(field[1]) + slope_depth(field[2])


def heavy_slopes(level):
    heavy = 0.5 * (1.0 + jnp.tanh(level))
    return jnp.stack([slope_line(heavy), slope_span(heavy), slope_depth(heavy)])


MESH = pl.DeviceIdType.MESH


def halves(table):
    high = table.astype(np.float32).astype(ml_dtypes.bfloat16)
    low = (table - high.astype(np.float64)).astype(np.float32).astype(ml_dtypes.bfloat16)
    return np.stack([high, low])


def line_tables(line, peers):
    position = np.arange(line)[:, None]
    wavenum = np.arange(line // 2)[None, :]
    phase = (position * wavenum % line) * (2.0 * math.pi / line)
    nyquist = np.where(position % 2 == 0, 1.0, -1.0)
    second = np.where(wavenum == 0, nyquist, -np.sin(phase))
    table = np.stack([np.cos(phase), second], axis=1) / math.sqrt(line)
    own = line // 2 // peers
    table = table.reshape(line, 2, peers, own).transpose(2, 0, 1, 3).reshape(peers, line, 2 * own)
    table = table.reshape(peers // 2, 2, line, 2 * own).transpose(0, 2, 1, 3)
    return halves(table.reshape(peers // 2, line, 4 * own))


def span_tables(span):
    index = np.arange(span)
    phase = (index[:, None] * index[None, :] % span) * (2.0 * math.pi / span)
    return halves(np.concatenate([np.cos(phase), np.sin(phase)], axis=1) / math.sqrt(span))


def split(value):
    high = value.astype(jnp.bfloat16)
    return high, (value - high.astype(jnp.float32)).astype(jnp.bfloat16)


def dot3(left, high, low):
    rows = left.shape[0]
    first, rest = split(left)
    both = jnp.dot(jnp.concatenate([first, rest], axis=0), high, preferred_element_type=jnp.float32)
    return both[:rows] + both[rows:] + jnp.dot(first, low, preferred_element_type=jnp.float32)


def rolled(value, step, axis):
    return pltpu.roll(value, (-step) % value.shape[axis], axis)


def rise(value, axis):
    return rolled(value, 1, axis) - rolled(value, -1, axis)


def whole_kernel(
    peers, slabs, level_hbm, vel_hbm, line_hbm, span_hbm, force_ref, out_ref,
    line_tab, span_tab, lev, vel_x, vel_y, vel_z, nor_x, nor_y, nor_z, act, mix_x, mix_y, mix_z,
    lhs, pack, edge, corner_out, corner_in, sent, got,
    load_sem, edge_send, edge_recv, corner_send, corner_recv, deep_send, deep_recv, vz_send, vz_recv, send_sem, recv_sem,
):
    me = lax.axis_index("gy")
    slab = lax.axis_index("gz")
    chips = peers // 2
    chip = me // 2
    core = me % 2
    depth, span, line = level_hbm.shape
    wide = span + 8
    chunks = depth // 2

    def place(dy, dz):
        return {"gy": (me + dy) % peers, "gz": (slab + dz) % slabs}

    loads = [
        pltpu.make_async_copy(level_hbm, lev.at[pl.ds(3, depth), pl.ds(0, span)], load_sem.at[0]),
        pltpu.make_async_copy(vel_hbm.at[1], vel_y.at[:, pl.ds(0, span)], load_sem.at[1]),
        pltpu.make_async_copy(vel_hbm.at[2], vel_z.at[pl.ds(1, depth)], load_sem.at[2]),
        pltpu.make_async_copy(vel_hbm.at[0], vel_x, load_sem.at[3]),
        pltpu.make_async_copy(line_hbm, line_tab, load_sem.at[4]),
        pltpu.make_async_copy(span_hbm, span_tab, load_sem.at[5]),
    ]
    for load in loads:
        load.start()

    greeted = {(off, 0) for off in range(1, peers)}
    greeted |= {(dy % peers, dz % slabs) for dy in (-1, 0, 1) for dz in (-1, 1)}
    barrier = pltpu.get_barrier_semaphore()
    for dy, dz in sorted(greeted):
        pl.semaphore_signal(barrier, inc=1, device_id=place(dy, dz), device_id_type=MESH)
    pl.semaphore_wait(barrier, len(greeted))

    def remote(src, dst, send, recv, target):
        return pltpu.make_async_remote_copy(
            src_ref=src, dst_ref=dst, send_sem=send, recv_sem=recv, device_id=target, device_id_type=MESH)

    deep = {}
    for near in range(1, 4):
        deep[near] = [
            remote(level_hbm.at[near - 1], lev.at[depth + 2 + near, pl.ds(0, span)],
                   deep_send.at[near - 1, 0], deep_recv.at[near - 1, 0], place(0, -1)),
            remote(level_hbm.at[depth - near], lev.at[3 - near, pl.ds(0, span)],
                   deep_send.at[near - 1, 1], deep_recv.at[near - 1, 1], place(0, 1)),
        ]
    deep_vel = [
        remote(vel_hbm.at[2, 0], vel_z.at[depth + 1], vz_send.at[0], vz_recv.at[0], place(0, -1)),
        remote(vel_hbm.at[2, depth - 1], vel_z.at[0], vz_send.at[1], vz_recv.at[1], place(0, 1)),
    ]
    edges = [
        remote(pack.at[side], edge.at[side], edge_send.at[side], edge_recv.at[side], place(2 * side - 1, 0))
        for side in range(2)
    ]
    corners = [
        remote(corner_out.at[i], corner_in.at[i], corner_send.at[i], corner_recv.at[i],
               place(2 * (i % 2) - 1, 2 * (i // 2) - 1))
        for i in range(4)
    ]
    for copy in deep[1]:
        copy.start()
    loads[0].wait()
    loads[1].wait()
    for layer in range(depth):
        pack[0, layer, 0:3] = lev[3 + layer, 0:3]
        pack[0, layer, 3:4] = vel_y[layer, 0:1]
        pack[1, layer, 0:3] = lev[3 + layer, span - 3:span]
        pack[1, layer, 3:4] = vel_y[layer, span - 1:span]
    for copy in edges:
        copy.start()
    for i in range(4):
        first, second = ((3, 4), (depth + 2, depth + 1))[i // 2]
        if i % 2 == 0:
            corner_out[i, 0:2] = lev[first, 0:2]
            corner_out[i, 2:3] = lev[second, 0:1]
        else:
            corner_out[i, 0:2] = lev[first, span - 2:span]
            corner_out[i, 2:3] = lev[second, span - 1:span]
        corner_out[i, 3:4] = jnp.zeros((1, line), jnp.float32)
        corners[i].start()
    for near in (2, 3):
        for copy in deep[near]:
            copy.start()
    for copy in deep_vel:
        copy.start()
    loads[2].wait()
    loads[3].wait()
    for copy in edges:
        copy.wait_recv()
    for layer in range(depth):
        lev[3 + layer, span:span + 3] = edge[0, layer, 0:3]
        vel_y[layer, span:span + 1] = edge[0, layer, 3:4]
        lev[3 + layer, wide - 3:wide] = edge[1, layer, 0:3]
        vel_y[layer, wide - 1:wide] = edge[1, layer, 3:4]

    def normals(p):
        here = lev[p]
        dx = rise(here, 1)
        dy = rise(here, 0)
        dz = lev[p + 1] - lev[p - 1]
        scale = lax.rsqrt(dx * dx + dy * dy + dz * dz + 4.0)
        nor_x[p] = dx * scale
        nor_y[p] = dy * scale
        nor_z[p] = dz * scale
        act[p] = jnp.tanh(here)

    def forces(p, inner):
        bend = -0.125 * (rise(nor_x[p], 1) + rise(nor_y[p], 0) + nor_z[p + 1] - nor_z[p - 1])
        own = bend[:span]
        force_z = own * (act[p + 1, :span] - act[p - 1, :span])
        mix_z[p] = vel_z[p - 2] + time_step * force_z
        if inner:
            here = act[p]
            force_x = own * rise(here[:span], 1)
            force_y = bend * rise(here, 0)
            force_ref[0, p - 3] = force_x
            force_ref[1, p - 3] = force_y[:span]
            force_ref[2, p - 3] = force_z
            mix_x[p - 3] = vel_x[p - 3] + time_step * force_x
            mix_y[p - 3] = vel_y[p - 3] + time_step * force_y

    def source(p):
        return 0.5 * (rise(mix_x[p - 3], 1) + rise(mix_y[p - 3], 0)[:span] + mix_z[p + 1] - mix_z[p - 1])

    def each(first, last, ends_only, body):
        if ends_only:
            pl.loop(0, 2)(lambda i: body(first + i * (last - first)))
        else:
            pl.loop(first, last + 1)(body)

    for chunk in range(chunks):
        low = 2 + chunks - chunk
        high = 3 + chunks + chunk
        near = 6 - low
        if near >= 1:
            for copy in deep[near]:
                copy.wait_recv()
        if near == 1:
            for copy in corners:
                copy.wait_recv()
        if near in (1, 2):
            rows = 2 if near == 1 else 1
            begin = 0 if near == 1 else 2
            for i in range(4):
                layer = depth + 2 + near if i // 2 == 0 else 3 - near
                row = span if i % 2 == 0 else wide - rows
                lev[layer, row:row + rows] = corner_in[i, begin:begin + rows]
        each(low - 2, high + 2, chunk > 0, normals)
        if low == 3:
            for copy in deep_vel:
                copy.wait_recv()
        each(low - 1, high + 1, chunk > 0, functools.partial(forces, inner=low > 3))
        for i, p in enumerate((low, high)):
            first, rest = split(source(p))
            lhs[i * span:(i + 1) * span] = first
            lhs[(2 + i) * span:(3 + i) * span] = rest
        if chunk == 0:
            loads[4].wait()

        def transform(target):
            both = jnp.dot(lhs[...], line_tab[0, target], preferred_element_type=jnp.float32)
            block = both[:2 * span] + both[2 * span:] + jnp.dot(
                lhs[0:2 * span], line_tab[1, target], preferred_element_type=jnp.float32)
            half = block.shape[1] // 2
            return [block[:, side * half:(side + 1) * half].reshape(2, span, half) for side in range(2)]

        @pl.loop(0, chips - 1)
        def _(step):
            target = (chip + chips // 2 + step + step // (chips // 2)) % chips
            blocks = transform(target)
            for side in range(2):
                sent[chunk, step, side] = blocks[side]
                remote(sent.at[chunk, step, side], got.at[chunk, me], send_sem.at[chunk, step, side],
                       recv_sem.at[chunk, me], {"gy": 2 * target + side, "gz": slab}).start()

        blocks = transform(chip)
        for side in range(2):
            sent[chunk, chips - 1, side] = blocks[side]
        remote(sent.at[chunk, chips - 1, 1 - core], got.at[chunk, me], send_sem.at[chunk, chips - 1, 0],
               recv_sem.at[chunk, me], {"gy": 2 * chip + 1 - core, "gz": slab}).start()
        got[chunk, me] = sent[chunk, chips - 1, core]

    loads[5].wait()
    total = peers * span
    for chunk in range(chunks):
        @pl.loop(1, peers)
        def _(off):
            origin = (me + off) % peers
            remote(sent.at[chunk, 0, 0], got.at[chunk, origin], send_sem.at[chunk, 0, 0],
                   recv_sem.at[chunk, origin], {"gy": origin, "gz": slab}).wait_recv()
        for i, layer in enumerate((chunks - 1 - chunk, chunks + chunk)):
            lines = got[chunk, :, i].reshape(total, -1).T
            own = lines.shape[0] // 2
            product = dot3(lines, span_tab[0], span_tab[1])
            out_ref[layer, 0] = product[:own, :total] + product[own:, total:]
            out_ref[layer, 1] = product[own:, :total] - product[:own, total:]
    for copy in deep[1] + deep[2] + deep[3] + deep_vel + edges + corners:
        copy.wait_send()
    for chunk in range(chunks):
        @pl.loop(0, chips - 1)
        def _(step):
            for side in range(2):
                remote(sent.at[chunk, step, side], got.at[chunk, me], send_sem.at[chunk, step, side],
                       recv_sem.at[chunk, me], {"gy": (me + 1) % peers, "gz": slab}).wait_send()
        remote(sent.at[chunk, chips - 1, 0], got.at[chunk, me], send_sem.at[chunk, chips - 1, 0],
               recv_sem.at[chunk, me], {"gy": (me + 1) % peers, "gz": slab}).wait_send()


def whole_by_kernel(level_set, velocity, peers, slabs):
    depth, span, line = level_set.shape
    own = line // 2 // peers
    wide = span + 8
    chunks = depth // 2
    vmem = pl.BlockSpec(memory_space=pltpu.VMEM)
    hbm = pl.BlockSpec(memory_space=pl.ANY)
    f32 = lambda *shape: pltpu.VMEM(shape, jnp.float32)
    dma = lambda *shape: pltpu.SemaphoreType.DMA(shape)
    return pl.pallas_call(
        functools.partial(whole_kernel, peers, slabs),
        out_shape=(
            jax.ShapeDtypeStruct((3, depth, span, line), jnp.float32),
            jax.ShapeDtypeStruct((depth, 2, own, peers * span), jnp.float32),
        ),
        in_specs=[hbm, hbm, hbm, hbm],
        out_specs=(vmem, vmem),
        scratch_shapes=[
            pltpu.VMEM((2, peers // 2, line, 4 * own), jnp.bfloat16),
            pltpu.VMEM((2, peers * span, 2 * peers * span), jnp.bfloat16),
            f32(depth + 6, wide, line),
            f32(depth, span, line),
            f32(depth, wide, line),
            f32(depth + 2, span, line),
            f32(depth + 6, wide, line),
            f32(depth + 6, wide, line),
            f32(depth + 6, wide, line),
            f32(depth + 6, wide, line),
            f32(depth, span, line),
            f32(depth, wide, line),
            f32(depth + 6, span, line),
            pltpu.VMEM((4 * span, line), jnp.bfloat16),
            f32(2, depth, 4, line),
            f32(2, depth, 4, line),
            f32(4, 4, line),
            f32(4, 4, line),
            f32(chunks, peers // 2, 2, 2, span, 2 * own),
            f32(chunks, peers, 2, span, 2 * own),
            dma(6), dma(2), dma(2), dma(4), dma(4), dma(3, 2), dma(3, 2), dma(2), dma(2),
            dma(chunks, peers // 2, 2), dma(chunks, peers),
        ],
        compiler_params=pltpu.CompilerParams(
            collective_id=0, has_side_effects=True, vmem_limit_bytes=58 * 2**20),
    )(level_set, velocity, jnp.asarray(line_tables(line, peers)), jnp.asarray(span_tables(peers * span)))


def on_device(level_set, velocity):
    peers, slabs = lax.axis_size("gy"), lax.axis_size("gz")
    depth, span, line = level_set.shape
    if peers % 4 == 0 and slabs > 1 and line == 128 * peers and span % 16 == 0 and depth % 2 == 0 and depth >= 8:
        return whole_by_kernel(level_set, velocity, peers, slabs)
    padded = padded_2(level_set, (("gy", 1), ("gz", 0)), 3)
    vel_wide = padded_2(velocity, (("gy", 2), ("gz", 1)), 1)
    kappa = -divergence(normals_from(padded))
    force_wide = surface_tension * kappa * heavy_slopes(padded[1:-1, 1:-1])
    force_own = force_wide[:, 1:-1, 1:-1]
    div_force = divergence(force_wide)
    source = divergence(vel_wide) + time_step * div_force
    depth_cells = source.shape[0]
    span_cells = source.shape[1]
    half_len = X // 2
    span_total = span_cells * lax.axis_size("gy")
    position = jnp.arange(X, dtype=jnp.int32)[:, None]
    wavenum = jnp.arange(half_len, dtype=jnp.int32)[None, :]
    phase = (position * wavenum % X).astype(jnp.float32) * (2.0 * math.pi / X)
    nyquist = jnp.where(position % 2 == 0, 1.0, -1.0).astype(jnp.float32)
    second = jnp.where(wavenum == 0, nyquist, -jnp.sin(phase))
    line_table = (jnp.stack([jnp.cos(phase), second], axis=1) / math.sqrt(X)).reshape(X, X)
    transformed = jnp.dot(
        source.reshape(-1, X),
        line_table,
        precision=lax.Precision.HIGHEST,
        preferred_element_type=jnp.float32,
    )
    transformed = transformed.reshape(depth_cells, span_cells, 2, half_len)
    rows_index = jnp.arange(span_total, dtype=jnp.int32)[:, None]
    cols_index = jnp.arange(span_total, dtype=jnp.int32)[None, :]
    span_phase = (rows_index * cols_index % span_total).astype(jnp.float32) * (
        2.0 * math.pi / span_total
    )
    span_cos = jnp.cos(span_phase) / math.sqrt(span_total)
    span_sin = jnp.sin(span_phase) / math.sqrt(span_total)
    piece = lax.all_to_all(transformed, "gy", split_axis=3, concat_axis=1, tiled=True)
    first = piece[:, :, 0, :]
    other = piece[:, :, 1, :]
    high = lax.Precision.HIGHEST
    first_cos = jnp.einsum("nyk,yq->nkq", first, span_cos, precision=high)
    first_sin = jnp.einsum("nyk,yq->nkq", first, span_sin, precision=high)
    other_cos = jnp.einsum("nyk,yq->nkq", other, span_cos, precision=high)
    other_sin = jnp.einsum("nyk,yq->nkq", other, span_sin, precision=high)
    spectrum = jnp.stack([first_cos + other_sin, other_cos - first_sin], axis=1)
    return (force_own, spectrum)


def solution(mesh):
    placed = (P("gz", "gy", None), P(None, "gz", "gy", None))
    return jax.shard_map(
        on_device,
        mesh=mesh,
        in_specs=placed,
        out_specs=(P(None, "gz", "gy", None), P("gz", None, "gy", None)),
        check_vma=False,
    )
```

```python
import functools
import math

import jax
import jax.numpy as jnp
import ml_dtypes
import numpy as np
from jax import lax
from jax.experimental import pallas as pl
from jax.experimental.pallas import tpu as pltpu
from jax.sharding import PartitionSpec as P

X = 2048


surface_tension = 1.0
time_step = 0.5


def padded_2(cells, sides, width):
    for axis, dim in sides:
        count = lax.axis_size(axis)
        head = lax.slice_in_dim(cells, 0, width, axis=dim)
        tail = lax.slice_in_dim(cells, cells.shape[dim] - width, cells.shape[dim], axis=dim)
        cells = jnp.concatenate(
            [
                lax.ppermute(tail, axis, [(i, (i + 1) % count) for i in range(count)]),
                cells,
                lax.ppermute(head, axis, [((i + 1) % count, i) for i in range(count)]),
            ],
            axis=dim,
        )
    return cells


def slope_depth(field):
    return (field[..., 2:, 1:-1, :] - field[..., :-2, 1:-1, :]) * 0.5


def slope_span(field):
    return (field[..., 1:-1, 2:, :] - field[..., 1:-1, :-2, :]) * 0.5


def slope_line(field):
    inner = field[..., 1:-1, 1:-1, :]
    return (jnp.roll(inner, -1, -1) - jnp.roll(inner, 1, -1)) * 0.5


def normals_from(level):
    grad_x = slope_line(level)
    grad_y = slope_span(level)
    grad_z = slope_depth(level)
    scale = jnp.sqrt(grad_x * grad_x + grad_y * grad_y + grad_z * grad_z + 1.0)
    return jnp.stack([grad_x / scale, grad_y / scale, grad_z / scale])


def divergence(field):
    return slope_line(field[0]) + slope_span(field[1]) + slope_depth(field[2])


def heavy_slopes(level):
    heavy = 0.5 * (1.0 + jnp.tanh(level))
    return jnp.stack([slope_line(heavy), slope_span(heavy), slope_depth(heavy)])


MESH = pl.DeviceIdType.MESH


def halves(table):
    high = table.astype(np.float32).astype(ml_dtypes.bfloat16)
    low = (table - high.astype(np.float64)).astype(np.float32).astype(ml_dtypes.bfloat16)
    return np.stack([high, low])


def line_tables(line, peers):
    position = np.arange(line // 2)[:, None]
    wavenum = np.arange(line // 2)[None, :]
    phase = (position * wavenum % line) * (2.0 * math.pi / line)
    nyquist = np.where(position % 2 == 0, 1.0, -1.0)
    second = np.where(wavenum == 0, nyquist, -np.sin(phase))
    table = np.stack([np.cos(phase), second], axis=1) / math.sqrt(line)
    own = line // 2 // peers
    table = table.reshape(line // 2, 2, peers // 4, 4, own // 2, 2).transpose(2, 5, 0, 3, 1, 4)
    return halves(table.reshape(peers // 4, 2, line // 2, 4 * own))


def span_tables(span):
    index = np.arange(span)
    phase = (index[:, None] * index[None, :] % span) * (2.0 * math.pi / span)
    return halves(np.concatenate([np.cos(phase), np.sin(phase)], axis=1) / math.sqrt(span))


def split(value):
    high = value.astype(jnp.bfloat16)
    return high, (value - high.astype(jnp.float32)).astype(jnp.bfloat16)


def dot3(left, high, low):
    rows = left.shape[0]
    first, rest = split(left)
    both = jnp.dot(jnp.concatenate([first, rest], axis=0), high, preferred_element_type=jnp.float32)
    return both[:rows] + both[rows:] + jnp.dot(first, low, preferred_element_type=jnp.float32)


def rolled(value, step, axis):
    return pltpu.roll(value, (-step) % value.shape[axis], axis)


def rise(value, axis):
    return rolled(value, 1, axis) - rolled(value, -1, axis)


def whole_kernel(
    peers, slabs, level_hbm, vel_hbm, line_hbm, span_hbm, force_ref, out_ref,
    line_tab, span_tab, lev, vel_x, vel_y, vel_z, nor_x, nor_y, nor_z, act, mix_x, mix_y, mix_z,
    lhs, pack, edge, corner_out, corner_in, sent, got, interim,
    load_sem, edge_send, edge_recv, corner_send, corner_recv, deep_send, deep_recv, vz_send, vz_recv, send_sem, recv_sem,
):
    me = lax.axis_index("gy")
    slab = lax.axis_index("gz")
    fours = peers // 4
    four = me // 4
    mine = me % 4
    depth, span, line = level_hbm.shape
    wide = span + 8
    chunks = depth // 2

    def place(dy, dz):
        return {"gy": (me + dy) % peers, "gz": (slab + dz) % slabs}

    loads = [
        pltpu.make_async_copy(level_hbm, lev.at[pl.ds(3, depth), pl.ds(0, span)], load_sem.at[0]),
        pltpu.make_async_copy(vel_hbm.at[1], vel_y.at[:, pl.ds(0, span)], load_sem.at[1]),
        pltpu.make_async_copy(vel_hbm.at[2], vel_z.at[pl.ds(1, depth)], load_sem.at[2]),
        pltpu.make_async_copy(vel_hbm.at[0], vel_x, load_sem.at[3]),
        pltpu.make_async_copy(line_hbm, line_tab, load_sem.at[4]),
        pltpu.make_async_copy(span_hbm, span_tab, load_sem.at[5]),
    ]
    for load in loads:
        load.start()

    greeted = {(off, 0) for off in range(1, peers)}
    greeted |= {(dy % peers, dz % slabs) for dy in (-1, 0, 1) for dz in (-1, 1)}
    barrier = pltpu.get_barrier_semaphore()
    for dy, dz in sorted(greeted):
        pl.semaphore_signal(barrier, inc=1, device_id=place(dy, dz), device_id_type=MESH)
    pl.semaphore_wait(barrier, len(greeted))

    def remote(src, dst, send, recv, target):
        return pltpu.make_async_remote_copy(
            src_ref=src, dst_ref=dst, send_sem=send, recv_sem=recv, device_id=target, device_id_type=MESH)

    deep = {}
    for near in range(1, 4):
        deep[near] = [
            remote(level_hbm.at[near - 1], lev.at[depth + 2 + near, pl.ds(0, span)],
                   deep_send.at[near - 1, 0], deep_recv.at[near - 1, 0], place(0, -1)),
            remote(level_hbm.at[depth - near], lev.at[3 - near, pl.ds(0, span)],
                   deep_send.at[near - 1, 1], deep_recv.at[near - 1, 1], place(0, 1)),
        ]
    deep_vel = [
        remote(vel_hbm.at[2, 0], vel_z.at[depth + 1], vz_send.at[0], vz_recv.at[0], place(0, -1)),
        remote(vel_hbm.at[2, depth - 1], vel_z.at[0], vz_send.at[1], vz_recv.at[1], place(0, 1)),
    ]
    edges = [
        remote(pack.at[side], edge.at[side], edge_send.at[side], edge_recv.at[side], place(2 * side - 1, 0))
        for side in range(2)
    ]
    corners = [
        remote(corner_out.at[i], corner_in.at[i], corner_send.at[i], corner_recv.at[i],
               place(2 * (i % 2) - 1, 2 * (i // 2) - 1))
        for i in range(4)
    ]
    for copy in deep[1]:
        copy.start()
    loads[0].wait()
    loads[1].wait()
    for layer in range(depth):
        pack[0, layer, 0:3] = lev[3 + layer, 0:3]
        pack[0, layer, 3:4] = vel_y[layer, 0:1]
        pack[1, layer, 0:3] = lev[3 + layer, span - 3:span]
        pack[1, layer, 3:4] = vel_y[layer, span - 1:span]
    for copy in edges:
        copy.start()
    for i in range(4):
        first, second = ((3, 4), (depth + 2, depth + 1))[i // 2]
        if i % 2 == 0:
            corner_out[i, 0:2] = lev[first, 0:2]
            corner_out[i, 2:3] = lev[second, 0:1]
        else:
            corner_out[i, 0:2] = lev[first, span - 2:span]
            corner_out[i, 2:3] = lev[second, span - 1:span]
        corner_out[i, 3:4] = jnp.zeros((1, line), jnp.float32)
        corners[i].start()
    for near in (2, 3):
        for copy in deep[near]:
            copy.start()
    for copy in deep_vel:
        copy.start()
    loads[2].wait()
    loads[3].wait()
    for copy in edges:
        copy.wait_recv()
    for layer in range(depth):
        lev[3 + layer, span:span + 3] = edge[0, layer, 0:3]
        vel_y[layer, span:span + 1] = edge[0, layer, 3:4]
        lev[3 + layer, wide - 3:wide] = edge[1, layer, 0:3]
        vel_y[layer, wide - 1:wide] = edge[1, layer, 3:4]

    def normals(p):
        here = lev[p]
        dx = rise(here, 1)
        dy = rise(here, 0)
        dz = lev[p + 1] - lev[p - 1]
        scale = lax.rsqrt(dx * dx + dy * dy + dz * dz + 4.0)
        nor_x[p] = dx * scale
        nor_y[p] = dy * scale
        nor_z[p] = dz * scale
        act[p] = jnp.tanh(here)

    def forces(p, inner):
        bend = -0.125 * (rise(nor_x[p], 1) + rise(nor_y[p], 0) + nor_z[p + 1] - nor_z[p - 1])
        own = bend[:span]
        force_z = own * (act[p + 1, :span] - act[p - 1, :span])
        mix_z[p] = vel_z[p - 2] + time_step * force_z
        if inner:
            here = act[p]
            force_x = own * rise(here[:span], 1)
            force_y = bend * rise(here, 0)
            force_ref[0, p - 3] = force_x
            force_ref[1, p - 3] = force_y[:span]
            force_ref[2, p - 3] = force_z
            mix_x[p - 3] = vel_x[p - 3] + time_step * force_x
            mix_y[p - 3] = vel_y[p - 3] + time_step * force_y

    def source(p):
        return 0.5 * (rise(mix_x[p - 3], 1) + rise(mix_y[p - 3], 0)[:span] + mix_z[p + 1] - mix_z[p - 1])

    def each(first, last, ends_only, body):
        if ends_only:
            pl.loop(0, 2)(lambda i: body(first + i * (last - first)))
        else:
            pl.loop(first, last + 1)(body)

    for chunk in range(chunks):
        low = 2 + chunks - chunk
        high = 3 + chunks + chunk
        near = 6 - low
        if near >= 1:
            for copy in deep[near]:
                copy.wait_recv()
        if near == 1:
            for copy in corners:
                copy.wait_recv()
        if near in (1, 2):
            rows = 2 if near == 1 else 1
            begin = 0 if near == 1 else 2
            for i in range(4):
                layer = depth + 2 + near if i // 2 == 0 else 3 - near
                row = span if i % 2 == 0 else wide - rows
                lev[layer, row:row + rows] = corner_in[i, begin:begin + rows]
        each(low - 2, high + 2, chunk > 0, normals)
        if low == 3:
            for copy in deep_vel:
                copy.wait_recv()
        each(low - 1, high + 1, chunk > 0, functools.partial(forces, inner=low > 3))
        for i, p in enumerate((low, high)):
            cells = source(p)
            for parity in range(2):
                near_half, far_half = cells[:, :line // 2], cells[:, line // 2:]
                first, rest = split(near_half - far_half if parity else near_half + far_half)
                lhs[parity, i * span:(i + 1) * span] = first
                lhs[parity, (2 + i) * span:(3 + i) * span] = rest
        if chunk == 0:
            loads[4].wait()

        def transform(target):
            pair = []
            for parity in range(2):
                both = jnp.dot(lhs[parity], line_tab[0, target, parity], preferred_element_type=jnp.float32)
                pair.append(both[:2 * span] + both[2 * span:] + jnp.dot(
                    lhs[parity, 0:2 * span], line_tab[1, target, parity], preferred_element_type=jnp.float32))
            width = pair[0].shape[1] // 2
            in_front = lax.broadcasted_iota(jnp.int32, (2 * span, width), 1) < width // 2
            blocks = []
            for part in range(2):
                even, odd = (value[:, part * width:(part + 1) * width] for value in pair)
                blocks.append(jnp.where(in_front, even, pltpu.roll(odd, width // 2, 1)))
                blocks.append(jnp.where(in_front, pltpu.roll(even, width // 2, 1), odd))
            return [block.reshape(2, span, width) for block in blocks]

        def send(step, slot, target):
            return remote(sent.at[chunk, step, slot], got.at[chunk, me], send_sem.at[chunk, step, slot],
                          recv_sem.at[chunk, me], {"gy": target, "gz": slab})

        @pl.loop(0, fours - 1)
        def _(step):
            target = (four + fours // 2 + step + step // (fours // 2)) % fours
            blocks = transform(target)
            for slot in range(4):
                sent[chunk, step, slot] = blocks[slot]
                send(step, slot, 4 * target + slot).start()

        blocks = transform(four)
        for slot in range(4):
            sent[chunk, fours - 1, slot] = blocks[slot]
        for off in range(1, 4):
            slot = (mine + off) % 4
            send(fours - 1, slot, 4 * four + slot).start()
        got[chunk, me] = sent[chunk, fours - 1, mine]

    loads[5].wait()
    total = peers * span
    for chunk in range(chunks):
        @pl.loop(1, peers)
        def _(off):
            origin = (me + off) % peers
            remote(sent.at[chunk, 0, 0], got.at[chunk, origin], send_sem.at[chunk, 0, 0],
                   recv_sem.at[chunk, origin], {"gy": origin, "gz": slab}).wait_recv()
        for i, layer in enumerate((chunks - 1 - chunk, chunks + chunk)):
            lines = got[chunk, :, i].reshape(total, -1).T
            own = lines.shape[0] // 4
            product = dot3(lines, span_tab[0], span_tab[1])
            for parity in range(2):
                real = product[2 * own * parity:2 * own * parity + own]
                imag = product[2 * own * parity + own:2 * own * (parity + 1)]
                rows = pl.ds(parity, own, stride=2)
                for lane in range(0, total, 128):
                    turn = slice(total + lane, total + lane + 128)
                    cols = slice(lane, lane + 128)
                    interim[0, lane // 128, rows] = real[:, cols] + imag[:, turn]
                    interim[1, lane // 128, rows] = imag[:, cols] - real[:, turn]
            for part in range(2):
                for lane in range(0, total, 128):
                    out_ref[layer, part, :, lane:lane + 128] = interim[part, lane // 128]
    for copy in deep[1] + deep[2] + deep[3] + deep_vel + edges + corners:
        copy.wait_send()
    for chunk in range(chunks):
        @pl.loop(0, fours - 1)
        def _(step):
            for slot in range(4):
                remote(sent.at[chunk, step, slot], got.at[chunk, me], send_sem.at[chunk, step, slot],
                       recv_sem.at[chunk, me], {"gy": (me + 1) % peers, "gz": slab}).wait_send()
        for off in range(1, 4):
            slot = (mine + off) % 4
            remote(sent.at[chunk, fours - 1, slot], got.at[chunk, me], send_sem.at[chunk, fours - 1, slot],
                   recv_sem.at[chunk, me], {"gy": (me + 1) % peers, "gz": slab}).wait_send()


def settle_kernel(force_in, spec_in, force_out, spec_out, force_mem, spec_mem, in_sem, out_sem):
    ways = []
    for part in range(force_in.shape[0]):
        for piece in range(2):
            size = force_in.shape[1] // 2
            ways.append((force_in, force_mem, force_out, (part, pl.ds(piece * size, size))))
    for piece in range(2):
        size = spec_in.shape[0] // 2
        ways.append((spec_in, spec_mem, spec_out, (pl.ds(piece * size, size),)))
    ins = [pltpu.make_async_copy(a.at[at], b.at[at], in_sem.at[i]) for i, (a, b, c, at) in enumerate(ways)]
    outs = [pltpu.make_async_copy(b.at[at], c.at[at], out_sem.at[i]) for i, (a, b, c, at) in enumerate(ways)]
    for copy in ins:
        copy.start()
    for first, then in zip(ins, outs):
        first.wait()
        then.start()
    for copy in outs:
        copy.wait()


def settle(force, spec):
    hbm = pl.BlockSpec(memory_space=pl.ANY)
    return pl.pallas_call(
        settle_kernel,
        out_shape=(jax.ShapeDtypeStruct(force.shape, force.dtype), jax.ShapeDtypeStruct(spec.shape, spec.dtype)),
        in_specs=[hbm, hbm],
        out_specs=(hbm, hbm),
        scratch_shapes=[
            pltpu.VMEM(force.shape, force.dtype),
            pltpu.VMEM(spec.shape, spec.dtype),
            pltpu.SemaphoreType.DMA((8,)),
            pltpu.SemaphoreType.DMA((8,)),
        ],
        compiler_params=pltpu.CompilerParams(vmem_limit_bytes=56 * 2**20),
    )(force, spec)


def whole_by_kernel(level_set, velocity, peers, slabs):
    depth, span, line = level_set.shape
    own = line // 2 // peers
    wide = span + 8
    chunks = depth // 2
    vmem = pl.BlockSpec(memory_space=pltpu.VMEM)
    hbm = pl.BlockSpec(memory_space=pl.ANY)
    f32 = lambda *shape: pltpu.VMEM(shape, jnp.float32)
    dma = lambda *shape: pltpu.SemaphoreType.DMA(shape)
    return pl.pallas_call(
        functools.partial(whole_kernel, peers, slabs),
        out_shape=(
            jax.ShapeDtypeStruct((3, depth, span, line), jnp.float32),
            jax.ShapeDtypeStruct((depth, 2, own, peers * span), jnp.float32),
        ),
        in_specs=[hbm, hbm, hbm, hbm],
        out_specs=(vmem, vmem),
        scratch_shapes=[
            pltpu.VMEM((2, peers // 4, 2, line // 2, 4 * own), jnp.bfloat16),
            pltpu.VMEM((2, peers * span, 2 * peers * span), jnp.bfloat16),
            f32(depth + 6, wide, line),
            f32(depth, span, line),
            f32(depth, wide, line),
            f32(depth + 2, span, line),
            f32(depth + 6, wide, line),
            f32(depth + 6, wide, line),
            f32(depth + 6, wide, line),
            f32(depth + 6, wide, line),
            f32(depth, span, line),
            f32(depth, wide, line),
            f32(depth + 6, span, line),
            pltpu.VMEM((2, 4 * span, line // 2), jnp.bfloat16),
            f32(2, depth, 4, line),
            f32(2, depth, 4, line),
            f32(4, 4, line),
            f32(4, 4, line),
            f32(chunks, peers // 4, 4, 2, span, 2 * own),
            f32(chunks, peers, 2, span, 2 * own),
            f32(2, peers * span // 128, own, 128),
            dma(6), dma(2), dma(2), dma(4), dma(4), dma(3, 2), dma(3, 2), dma(2), dma(2),
            dma(chunks, peers // 4, 4), dma(chunks, peers),
        ],
        compiler_params=pltpu.CompilerParams(
            collective_id=0, has_side_effects=True, vmem_limit_bytes=58 * 2**20),
    )(level_set, velocity, jnp.asarray(line_tables(line, peers)), jnp.asarray(span_tables(peers * span)))


def on_device(level_set, velocity):
    peers, slabs = lax.axis_size("gy"), lax.axis_size("gz")
    depth, span, line = level_set.shape
    if peers % 8 == 0 and slabs > 1 and line == 128 * peers and span % 16 == 0 and depth % 2 == 0 and depth >= 8:
        return settle(*whole_by_kernel(level_set, velocity, peers, slabs))
    padded = padded_2(level_set, (("gy", 1), ("gz", 0)), 3)
    vel_wide = padded_2(velocity, (("gy", 2), ("gz", 1)), 1)
    kappa = -divergence(normals_from(padded))
    force_wide = surface_tension * kappa * heavy_slopes(padded[1:-1, 1:-1])
    force_own = force_wide[:, 1:-1, 1:-1]
    div_force = divergence(force_wide)
    source = divergence(vel_wide) + time_step * div_force
    depth_cells = source.shape[0]
    span_cells = source.shape[1]
    half_len = X // 2
    span_total = span_cells * lax.axis_size("gy")
    position = jnp.arange(X, dtype=jnp.int32)[:, None]
    wavenum = jnp.arange(half_len, dtype=jnp.int32)[None, :]
    phase = (position * wavenum % X).astype(jnp.float32) * (2.0 * math.pi / X)
    nyquist = jnp.where(position % 2 == 0, 1.0, -1.0).astype(jnp.float32)
    second = jnp.where(wavenum == 0, nyquist, -jnp.sin(phase))
    line_table = (jnp.stack([jnp.cos(phase), second], axis=1) / math.sqrt(X)).reshape(X, X)
    transformed = jnp.dot(
        source.reshape(-1, X),
        line_table,
        precision=lax.Precision.HIGHEST,
        preferred_element_type=jnp.float32,
    )
    transformed = transformed.reshape(depth_cells, span_cells, 2, half_len)
    rows_index = jnp.arange(span_total, dtype=jnp.int32)[:, None]
    cols_index = jnp.arange(span_total, dtype=jnp.int32)[None, :]
    span_phase = (rows_index * cols_index % span_total).astype(jnp.float32) * (
        2.0 * math.pi / span_total
    )
    span_cos = jnp.cos(span_phase) / math.sqrt(span_total)
    span_sin = jnp.sin(span_phase) / math.sqrt(span_total)
    piece = lax.all_to_all(transformed, "gy", split_axis=3, concat_axis=1, tiled=True)
    first = piece[:, :, 0, :]
    other = piece[:, :, 1, :]
    high = lax.Precision.HIGHEST
    first_cos = jnp.einsum("nyk,yq->nkq", first, span_cos, precision=high)
    first_sin = jnp.einsum("nyk,yq->nkq", first, span_sin, precision=high)
    other_cos = jnp.einsum("nyk,yq->nkq", other, span_cos, precision=high)
    other_sin = jnp.einsum("nyk,yq->nkq", other, span_sin, precision=high)
    spectrum = jnp.stack([first_cos + other_sin, other_cos - first_sin], axis=1)
    return (force_own, spectrum)


def solution(mesh):
    placed = (P("gz", "gy", None), P(None, "gz", "gy", None))
    return jax.shard_map(
        on_device,
        mesh=mesh,
        in_specs=placed,
        out_specs=(P(None, "gz", "gy", None), P("gz", None, "gy", None)),
        check_vma=False,
    )
```

```python
import functools
import math

import jax
import jax.numpy as jnp
import ml_dtypes
import numpy as np
from jax import lax
from jax.experimental import pallas as pl
from jax.experimental.pallas import tpu as pltpu
from jax.sharding import PartitionSpec as P

X = 2048


surface_tension = 1.0
time_step = 0.5


def padded_2(cells, sides, width):
    for axis, dim in sides:
        count = lax.axis_size(axis)
        head = lax.slice_in_dim(cells, 0, width, axis=dim)
        tail = lax.slice_in_dim(cells, cells.shape[dim] - width, cells.shape[dim], axis=dim)
        cells = jnp.concatenate(
            [
                lax.ppermute(tail, axis, [(i, (i + 1) % count) for i in range(count)]),
                cells,
                lax.ppermute(head, axis, [((i + 1) % count, i) for i in range(count)]),
            ],
            axis=dim,
        )
    return cells


def slope_depth(field):
    return (field[..., 2:, 1:-1, :] - field[..., :-2, 1:-1, :]) * 0.5


def slope_span(field):
    return (field[..., 1:-1, 2:, :] - field[..., 1:-1, :-2, :]) * 0.5


def slope_line(field):
    inner = field[..., 1:-1, 1:-1, :]
    return (jnp.roll(inner, -1, -1) - jnp.roll(inner, 1, -1)) * 0.5


def normals_from(level):
    grad_x = slope_line(level)
    grad_y = slope_span(level)
    grad_z = slope_depth(level)
    scale = jnp.sqrt(grad_x * grad_x + grad_y * grad_y + grad_z * grad_z + 1.0)
    return jnp.stack([grad_x / scale, grad_y / scale, grad_z / scale])


def divergence(field):
    return slope_line(field[0]) + slope_span(field[1]) + slope_depth(field[2])


def heavy_slopes(level):
    heavy = 0.5 * (1.0 + jnp.tanh(level))
    return jnp.stack([slope_line(heavy), slope_span(heavy), slope_depth(heavy)])


MESH = pl.DeviceIdType.MESH


def halves(table):
    high = table.astype(np.float32).astype(ml_dtypes.bfloat16)
    low = (table - high.astype(np.float64)).astype(np.float32).astype(ml_dtypes.bfloat16)
    return np.stack([high, low])


def line_tables(line, peers):
    position = np.arange(line // 2)[:, None]
    wavenum = np.arange(line // 2)[None, :]
    phase = (position * wavenum % line) * (2.0 * math.pi / line)
    nyquist = np.where(position % 2 == 0, 1.0, -1.0)
    second = np.where(wavenum == 0, nyquist, -np.sin(phase))
    table = np.stack([np.cos(phase), second], axis=1) / math.sqrt(line)
    own = line // 2 // peers
    table = table.reshape(line // 2, 2, peers // 4, 4, own // 2, 2).transpose(2, 5, 0, 3, 1, 4)
    return halves(table.reshape(peers // 4, 2, line // 2, 4 * own))


def span_tables(span):
    index = np.arange(span)
    phase = (index[:, None] * index[None, :] % span) * (2.0 * math.pi / span)
    return halves(np.concatenate([np.cos(phase), np.sin(phase)], axis=1) / math.sqrt(span))


def split(value):
    high = value.astype(jnp.bfloat16)
    return high, (value - high.astype(jnp.float32)).astype(jnp.bfloat16)


def dot3(left, high, low):
    rows = left.shape[0]
    first, rest = split(left)
    both = jnp.dot(jnp.concatenate([first, rest], axis=0), high, preferred_element_type=jnp.float32)
    return both[:rows] + both[rows:] + jnp.dot(first, low, preferred_element_type=jnp.float32)


def rolled(value, step, axis):
    return pltpu.roll(value, (-step) % value.shape[axis], axis)


def rise(value, axis):
    return rolled(value, 1, axis) - rolled(value, -1, axis)


def whole_kernel(
    peers, slabs, level_hbm, vel_hbm, line_hbm, span_hbm, force_ref, out_ref,
    line_tab, span_tab, lev, vel_x, vel_y, vel_z, nor_x, nor_y, nor_z, act, mix_x, mix_y, mix_z,
    lhs, pack, edge, corner_out, corner_in, sent, got, interim,
    load_sem, edge_send, edge_recv, corner_send, corner_recv, deep_send, deep_recv, mix_send, mix_recv, send_sem, recv_sem,
):
    me = lax.axis_index("gy")
    slab = lax.axis_index("gz")
    fours = peers // 4
    four = me // 4
    mine = me % 4
    depth, span, line = level_hbm.shape
    wide = span + 8
    chunks = depth // 2

    def place(dy, dz):
        return {"gy": (me + dy) % peers, "gz": (slab + dz) % slabs}

    loads = [
        pltpu.make_async_copy(level_hbm, lev.at[pl.ds(3, depth), pl.ds(0, span)], load_sem.at[0]),
        pltpu.make_async_copy(vel_hbm.at[1], vel_y.at[:, pl.ds(0, span)], load_sem.at[1]),
        pltpu.make_async_copy(vel_hbm.at[2], vel_z, load_sem.at[2]),
        pltpu.make_async_copy(vel_hbm.at[0], vel_x, load_sem.at[3]),
        pltpu.make_async_copy(line_hbm, line_tab, load_sem.at[4]),
        pltpu.make_async_copy(span_hbm, span_tab, load_sem.at[5]),
    ]
    for load in loads:
        load.start()

    greeted = {(off, 0) for off in range(1, peers)}
    greeted |= {(dy % peers, dz % slabs) for dy in (-1, 0, 1) for dz in (-1, 1)}
    barrier = pltpu.get_barrier_semaphore()
    for dy, dz in sorted(greeted):
        pl.semaphore_signal(barrier, inc=1, device_id=place(dy, dz), device_id_type=MESH)
    pl.semaphore_wait(barrier, len(greeted))

    def remote(src, dst, send, recv, target):
        return pltpu.make_async_remote_copy(
            src_ref=src, dst_ref=dst, send_sem=send, recv_sem=recv, device_id=target, device_id_type=MESH)

    deep = {}
    for near in range(1, 3):
        deep[near] = [
            remote(level_hbm.at[near - 1], lev.at[depth + 2 + near, pl.ds(0, span)],
                   deep_send.at[near - 1, 0], deep_recv.at[near - 1, 0], place(0, -1)),
            remote(level_hbm.at[depth - near], lev.at[3 - near, pl.ds(0, span)],
                   deep_send.at[near - 1, 1], deep_recv.at[near - 1, 1], place(0, 1)),
        ]
    deep_mix = [
        remote(mix_z.at[3], mix_z.at[depth + 3], mix_send.at[0], mix_recv.at[0], place(0, -1)),
        remote(mix_z.at[depth + 2], mix_z.at[2], mix_send.at[1], mix_recv.at[1], place(0, 1)),
    ]
    edges = [
        remote(pack.at[side], edge.at[side], edge_send.at[side], edge_recv.at[side], place(2 * side - 1, 0))
        for side in range(2)
    ]
    corners = [
        remote(corner_out.at[i], corner_in.at[i], corner_send.at[i], corner_recv.at[i],
               place(2 * (i % 2) - 1, 2 * (i // 2) - 1))
        for i in range(4)
    ]
    for copy in deep[1]:
        copy.start()
    loads[0].wait()
    loads[1].wait()
    for layer in range(depth):
        pack[0, layer, 0:3] = lev[3 + layer, 0:3]
        pack[0, layer, 3:4] = vel_y[layer, 0:1]
        pack[1, layer, 0:3] = lev[3 + layer, span - 3:span]
        pack[1, layer, 3:4] = vel_y[layer, span - 1:span]
    for copy in edges:
        copy.start()
    for i in range(4):
        first, second = ((3, 4), (depth + 2, depth + 1))[i // 2]
        if i % 2 == 0:
            corner_out[i, 0:2] = lev[first, 0:2]
            corner_out[i, 2:3] = lev[second, 0:1]
        else:
            corner_out[i, 0:2] = lev[first, span - 2:span]
            corner_out[i, 2:3] = lev[second, span - 1:span]
        corner_out[i, 3:4] = jnp.zeros((1, line), jnp.float32)
        corners[i].start()
    for copy in deep[2]:
        copy.start()
    loads[2].wait()
    loads[3].wait()
    for copy in edges:
        copy.wait_recv()
    for layer in range(depth):
        lev[3 + layer, span:span + 3] = edge[0, layer, 0:3]
        vel_y[layer, span:span + 1] = edge[0, layer, 3:4]
        lev[3 + layer, wide - 3:wide] = edge[1, layer, 0:3]
        vel_y[layer, wide - 1:wide] = edge[1, layer, 3:4]

    def normals(p):
        here = lev[p]
        dx = rise(here, 1)
        dy = rise(here, 0)
        dz = lev[p + 1] - lev[p - 1]
        scale = lax.rsqrt(dx * dx + dy * dy + dz * dz + 4.0)
        nor_x[p] = dx * scale
        nor_y[p] = dy * scale
        nor_z[p] = dz * scale
        act[p] = jnp.tanh(here)

    def forces(p):
        bend = -0.125 * (rise(nor_x[p], 1) + rise(nor_y[p], 0) + nor_z[p + 1] - nor_z[p - 1])
        own = bend[:span]
        force_z = own * (act[p + 1, :span] - act[p - 1, :span])
        here = act[p]
        force_x = own * rise(here[:span], 1)
        force_y = bend * rise(here, 0)
        force_ref[0, p - 3] = force_x
        force_ref[1, p - 3] = force_y[:span]
        force_ref[2, p - 3] = force_z
        mix_x[p - 3] = vel_x[p - 3] + time_step * force_x
        mix_y[p - 3] = vel_y[p - 3] + time_step * force_y
        mix_z[p] = vel_z[p - 3] + time_step * force_z

    def source(p):
        return 0.5 * (rise(mix_x[p - 3], 1) + rise(mix_y[p - 3], 0)[:span] + mix_z[p + 1] - mix_z[p - 1])

    def each(first, last, ends_only, body):
        if ends_only:
            pl.loop(0, 2)(lambda i: body(first + i * (last - first)))
        else:
            pl.loop(first, last + 1)(body)

    for chunk in range(chunks):
        low = 2 + chunks - chunk
        high = 3 + chunks + chunk
        near = 6 - low
        if near in (1, 2):
            for copy in deep[near]:
                copy.wait_recv()
        if near == 1:
            for copy in corners:
                copy.wait_recv()
        if near in (1, 2):
            rows = 2 if near == 1 else 1
            begin = 0 if near == 1 else 2
            for i in range(4):
                layer = depth + 2 + near if i // 2 == 0 else 3 - near
                row = span if i % 2 == 0 else wide - rows
                lev[layer, row:row + rows] = corner_in[i, begin:begin + rows]
        if low > 3:
            each(low - 2, high + 2, chunk > 0, normals)
            each(low - 1, high + 1, chunk > 0, forces)
        if low == 4:
            for copy in deep_mix:
                copy.start()
        if low == 3:
            for copy in deep_mix:
                copy.wait_recv()
        for i, p in enumerate((low, high)):
            cells = source(p)
            for parity in range(2):
                near_half, far_half = cells[:, :line // 2], cells[:, line // 2:]
                first, rest = split(near_half - far_half if parity else near_half + far_half)
                lhs[parity, i * span:(i + 1) * span] = first
                lhs[parity, (2 + i) * span:(3 + i) * span] = rest
        if chunk == 0:
            loads[4].wait()

        def transform(target):
            pair = []
            for parity in range(2):
                both = jnp.dot(lhs[parity], line_tab[0, target, parity], preferred_element_type=jnp.float32)
                pair.append(both[:2 * span] + both[2 * span:] + jnp.dot(
                    lhs[parity, 0:2 * span], line_tab[1, target, parity], preferred_element_type=jnp.float32))
            width = pair[0].shape[1] // 2
            in_front = lax.broadcasted_iota(jnp.int32, (2 * span, width), 1) < width // 2
            blocks = []
            for part in range(2):
                even, odd = (value[:, part * width:(part + 1) * width] for value in pair)
                blocks.append(jnp.where(in_front, even, pltpu.roll(odd, width // 2, 1)))
                blocks.append(jnp.where(in_front, pltpu.roll(even, width // 2, 1), odd))
            return [block.reshape(2, span, width) for block in blocks]

        def send(step, slot, target):
            return remote(sent.at[chunk, step, slot], got.at[chunk, me], send_sem.at[chunk, step, slot],
                          recv_sem.at[chunk, me], {"gy": target, "gz": slab})

        @pl.loop(0, fours - 1)
        def _(step):
            target = (four + fours // 2 + step + step // (fours // 2)) % fours
            blocks = transform(target)
            for slot in range(4):
                sent[chunk, step, slot] = blocks[slot]
                send(step, slot, 4 * target + slot).start()

        blocks = transform(four)
        for slot in range(4):
            sent[chunk, fours - 1, slot] = blocks[slot]
        for off in range(1, 4):
            slot = (mine + off) % 4
            send(fours - 1, slot, 4 * four + slot).start()
        got[chunk, me] = sent[chunk, fours - 1, mine]

    loads[5].wait()
    total = peers * span
    for chunk in range(chunks):
        @pl.loop(1, peers)
        def _(off):
            origin = (me + off) % peers
            remote(sent.at[chunk, 0, 0], got.at[chunk, origin], send_sem.at[chunk, 0, 0],
                   recv_sem.at[chunk, origin], {"gy": origin, "gz": slab}).wait_recv()
        for i, layer in enumerate((chunks - 1 - chunk, chunks + chunk)):
            lines = got[chunk, :, i].reshape(total, -1).T
            own = lines.shape[0] // 4
            product = dot3(lines, span_tab[0], span_tab[1])
            for parity in range(2):
                real = product[2 * own * parity:2 * own * parity + own]
                imag = product[2 * own * parity + own:2 * own * (parity + 1)]
                rows = pl.ds(parity, own, stride=2)
                for lane in range(0, total, 128):
                    turn = slice(total + lane, total + lane + 128)
                    cols = slice(lane, lane + 128)
                    interim[0, lane // 128, rows] = real[:, cols] + imag[:, turn]
                    interim[1, lane // 128, rows] = imag[:, cols] - real[:, turn]
            for part in range(2):
                for lane in range(0, total, 128):
                    out_ref[layer, part, :, lane:lane + 128] = interim[part, lane // 128]
    for copy in deep[1] + deep[2] + deep_mix + edges + corners:
        copy.wait_send()
    for chunk in range(chunks):
        @pl.loop(0, fours - 1)
        def _(step):
            for slot in range(4):
                remote(sent.at[chunk, step, slot], got.at[chunk, me], send_sem.at[chunk, step, slot],
                       recv_sem.at[chunk, me], {"gy": (me + 1) % peers, "gz": slab}).wait_send()
        for off in range(1, 4):
            slot = (mine + off) % 4
            remote(sent.at[chunk, fours - 1, slot], got.at[chunk, me], send_sem.at[chunk, fours - 1, slot],
                   recv_sem.at[chunk, me], {"gy": (me + 1) % peers, "gz": slab}).wait_send()


def settle_kernel(force_in, spec_in, force_out, spec_out, force_mem, spec_mem, in_sem, out_sem):
    ways = []
    for part in range(force_in.shape[0]):
        for piece in range(2):
            size = force_in.shape[1] // 2
            ways.append((force_in, force_mem, force_out, (part, pl.ds(piece * size, size))))
    for piece in range(2):
        size = spec_in.shape[0] // 2
        ways.append((spec_in, spec_mem, spec_out, (pl.ds(piece * size, size),)))
    ins = [pltpu.make_async_copy(a.at[at], b.at[at], in_sem.at[i]) for i, (a, b, c, at) in enumerate(ways)]
    outs = [pltpu.make_async_copy(b.at[at], c.at[at], out_sem.at[i]) for i, (a, b, c, at) in enumerate(ways)]
    for copy in ins:
        copy.start()
    for first, then in zip(ins, outs):
        first.wait()
        then.start()
    for copy in outs:
        copy.wait()


def settle(force, spec):
    hbm = pl.BlockSpec(memory_space=pl.ANY)
    return pl.pallas_call(
        settle_kernel,
        out_shape=(jax.ShapeDtypeStruct(force.shape, force.dtype), jax.ShapeDtypeStruct(spec.shape, spec.dtype)),
        in_specs=[hbm, hbm],
        out_specs=(hbm, hbm),
        scratch_shapes=[
            pltpu.VMEM(force.shape, force.dtype),
            pltpu.VMEM(spec.shape, spec.dtype),
            pltpu.SemaphoreType.DMA((8,)),
            pltpu.SemaphoreType.DMA((8,)),
        ],
        compiler_params=pltpu.CompilerParams(vmem_limit_bytes=56 * 2**20),
    )(force, spec)


def whole_by_kernel(level_set, velocity, peers, slabs):
    depth, span, line = level_set.shape
    own = line // 2 // peers
    wide = span + 8
    chunks = depth // 2
    vmem = pl.BlockSpec(memory_space=pltpu.VMEM)
    hbm = pl.BlockSpec(memory_space=pl.ANY)
    f32 = lambda *shape: pltpu.VMEM(shape, jnp.float32)
    dma = lambda *shape: pltpu.SemaphoreType.DMA(shape)
    return pl.pallas_call(
        functools.partial(whole_kernel, peers, slabs),
        out_shape=(
            jax.ShapeDtypeStruct((3, depth, span, line), jnp.float32),
            jax.ShapeDtypeStruct((depth, 2, own, peers * span), jnp.float32),
        ),
        in_specs=[hbm, hbm, hbm, hbm],
        out_specs=(vmem, vmem),
        scratch_shapes=[
            pltpu.VMEM((2, peers // 4, 2, line // 2, 4 * own), jnp.bfloat16),
            pltpu.VMEM((2, peers * span, 2 * peers * span), jnp.bfloat16),
            f32(depth + 6, wide, line),
            f32(depth, span, line),
            f32(depth, wide, line),
            f32(depth, span, line),
            f32(depth + 6, wide, line),
            f32(depth + 6, wide, line),
            f32(depth + 6, wide, line),
            f32(depth + 6, wide, line),
            f32(depth, span, line),
            f32(depth, wide, line),
            f32(depth + 6, span, line),
            pltpu.VMEM((2, 4 * span, line // 2), jnp.bfloat16),
            f32(2, depth, 4, line),
            f32(2, depth, 4, line),
            f32(4, 4, line),
            f32(4, 4, line),
            f32(chunks, peers // 4, 4, 2, span, 2 * own),
            f32(chunks, peers, 2, span, 2 * own),
            f32(2, peers * span // 128, own, 128),
            dma(6), dma(2), dma(2), dma(4), dma(4), dma(2, 2), dma(2, 2), dma(2), dma(2),
            dma(chunks, peers // 4, 4), dma(chunks, peers),
        ],
        compiler_params=pltpu.CompilerParams(
            collective_id=0, has_side_effects=True, vmem_limit_bytes=58 * 2**20),
    )(level_set, velocity, jnp.asarray(line_tables(line, peers)), jnp.asarray(span_tables(peers * span)))


def on_device(level_set, velocity):
    peers, slabs = lax.axis_size("gy"), lax.axis_size("gz")
    depth, span, line = level_set.shape
    if peers % 8 == 0 and slabs > 1 and line == 128 * peers and span % 16 == 0 and depth % 2 == 0 and depth >= 8:
        return settle(*whole_by_kernel(level_set, velocity, peers, slabs))
    padded = padded_2(level_set, (("gy", 1), ("gz", 0)), 3)
    vel_wide = padded_2(velocity, (("gy", 2), ("gz", 1)), 1)
    kappa = -divergence(normals_from(padded))
    force_wide = surface_tension * kappa * heavy_slopes(padded[1:-1, 1:-1])
    force_own = force_wide[:, 1:-1, 1:-1]
    div_force = divergence(force_wide)
    source = divergence(vel_wide) + time_step * div_force
    depth_cells = source.shape[0]
    span_cells = source.shape[1]
    half_len = X // 2
    span_total = span_cells * lax.axis_size("gy")
    position = jnp.arange(X, dtype=jnp.int32)[:, None]
    wavenum = jnp.arange(half_len, dtype=jnp.int32)[None, :]
    phase = (position * wavenum % X).astype(jnp.float32) * (2.0 * math.pi / X)
    nyquist = jnp.where(position % 2 == 0, 1.0, -1.0).astype(jnp.float32)
    second = jnp.where(wavenum == 0, nyquist, -jnp.sin(phase))
    line_table = (jnp.stack([jnp.cos(phase), second], axis=1) / math.sqrt(X)).reshape(X, X)
    transformed = jnp.dot(
        source.reshape(-1, X),
        line_table,
        precision=lax.Precision.HIGHEST,
        preferred_element_type=jnp.float32,
    )
    transformed = transformed.reshape(depth_cells, span_cells, 2, half_len)
    rows_index = jnp.arange(span_total, dtype=jnp.int32)[:, None]
    cols_index = jnp.arange(span_total, dtype=jnp.int32)[None, :]
    span_phase = (rows_index * cols_index % span_total).astype(jnp.float32) * (
        2.0 * math.pi / span_total
    )
    span_cos = jnp.cos(span_phase) / math.sqrt(span_total)
    span_sin = jnp.sin(span_phase) / math.sqrt(span_total)
    piece = lax.all_to_all(transformed, "gy", split_axis=3, concat_axis=1, tiled=True)
    first = piece[:, :, 0, :]
    other = piece[:, :, 1, :]
    high = lax.Precision.HIGHEST
    first_cos = jnp.einsum("nyk,yq->nkq", first, span_cos, precision=high)
    first_sin = jnp.einsum("nyk,yq->nkq", first, span_sin, precision=high)
    other_cos = jnp.einsum("nyk,yq->nkq", other, span_cos, precision=high)
    other_sin = jnp.einsum("nyk,yq->nkq", other, span_sin, precision=high)
    spectrum = jnp.stack([first_cos + other_sin, other_cos - first_sin], axis=1)
    return (force_own, spectrum)


def solution(mesh):
    placed = (P("gz", "gy", None), P(None, "gz", "gy", None))
    return jax.shard_map(
        on_device,
        mesh=mesh,
        in_specs=placed,
        out_specs=(P(None, "gz", "gy", None), P("gz", None, "gy", None)),
        check_vma=False,
    )
```
